32 devices in a mesh: row: 2 (over y), col: 16 (over z, x, core).
Axes of the slice: x: 2, y: 2, z: 4, core: 2. Of those that a mesh axis runs over, the one named last changes fastest.
Arguments:
- matrix: float32 [16384, 16384], P('row', 'col'), may hold values from -6 to 6
- reflectors: float32 [16384, 256], P(('row', 'col')), may hold values from -0.046875 to 0.046875
- factor: float32 [256, 256], replicated, may hold values from -0.375 to 0.375
Outputs:
- updated: float32 [16384, 16384], P('row', 'col')
- correction: float32 [16384, 256], P(('row', 'col'))
The draws below stay inside these ranges and needn't reach their ends.
All inputs are finite; a program needn't handle non-finite values.
Results may differ from the reference program's by a relative error of at most 0.000078.
Values sent between devices are 32-bit elements; how exact they have to be, the bound alone decides.
A program may use at most 192 MiB of HBM per device.

```python
import math
import jax
import jax.numpy as jnp
from jax import lax

N = 16384
B = 256


def draw_matrix(key, part):
    normal_draw = jax.random.normal(key, (N, N), jnp.float32)
    symmetric = (normal_draw + normal_draw.T) * math.sqrt(0.5)
    return jnp.clip(symmetric, -6.0, 6.0)


def steps_of(stream_key, extent, cuts, least, high):
    gain = 1.0
    for position, shards_of in cuts:
        heights = jax.random.uniform(jax.random.fold_in(jax.random.fold_in(stream_key, 6), position), (shards_of,), jnp.float32, least / len(cuts), high / len(cuts))
        gain = gain * jnp.repeat(jnp.exp(heights), extent[position] // shards_of).reshape((-1,) + (1,) * (len(extent) - 1 - position))
    return gain


def normal_values(key, extent, spread, reach, split=(), kind=jnp.bfloat16):
    drawn = spread * jax.random.normal(key, extent, jnp.float32)
    if split:
        drawn = drawn * steps_of(key, extent, split, -0.22, 0.18)
    return jnp.clip(drawn, -reach, reach).astype(kind)


def setup_inputs(seed: int = 0) -> dict:
    streams_of = jax.random.split(jax.random.key(seed), 4)
    matrix = draw_matrix(jax.random.fold_in(streams_of[3], 71), 0)
    reflectors = normal_values(streams_of[1], (N, B), N ** -0.5, 0.046875, ((0, 32),), jnp.float32)
    factor = normal_values(streams_of[2], (B, B), B ** -0.5, 0.375, (), jnp.float32)
    return dict(matrix=matrix, reflectors=reflectors, factor=factor)


def mult(left, right):
    return jnp.dot(left, right, precision=lax.Precision.HIGHEST, preferred_element_type=jnp.float32)


def reference(matrix, reflectors, factor):
    image = mult(matrix, reflectors)
    gram_matrix = mult(reflectors.T, image)
    inner = mult(mult(factor.T, gram_matrix), factor)
    correction = mult(image, factor) - 0.5 * mult(reflectors, inner)
    updated = matrix - mult(reflectors, correction.T) - mult(correction, reflectors.T)
    return updated, correction
```

```python
import functools

import jax
import jax.numpy as jnp
from jax import lax
from jax.experimental import pallas as pl
from jax.experimental.pallas import tpu as pltpu
from jax.sharding import PartitionSpec as P

F32 = jnp.float32
BF16 = jnp.bfloat16
VMEM_LIMIT = 48 * 1024 * 1024


def split(value):
    high = value.astype(BF16)
    return high, (value - high.astype(F32)).astype(BF16)


def dot(left, right):
    return jnp.dot(left, right, preferred_element_type=F32)


def dot3(left, right):
    (left_high, left_low), (right_high, right_low) = left, right
    return dot(left_high, right_high) + dot(left_low, right_high) + dot(left_high, right_low)


def mult(left, right, dims=((1,), (0,))):
    return lax.dot_general(
        left, right, (dims, ((), ())), precision=lax.Precision.HIGH, preferred_element_type=F32
    )


def image_kernel(matrix_ref, vec_ref, out_ref, total):
    step = pl.program_id(0)
    product = dot3(split(vec_ref[...].T), split(matrix_ref[...]))

    @pl.when(step == 0)
    def _():
        total[...] = product

    @pl.when(step > 0)
    def _():
        total[...] += product

    @pl.when(step == pl.num_programs(0) - 1)
    def _():
        out_ref[...] = total[...].T


def image_part(matrix, vec_rows):
    (rows, cols), width = matrix.shape, vec_rows.shape[1]
    block = min(512, rows)
    return pl.pallas_call(
        image_kernel,
        grid=(rows // block,),
        out_shape=jax.ShapeDtypeStruct((cols, width), F32),
        in_specs=[
            pl.BlockSpec((block, cols), lambda i: (i, 0)),
            pl.BlockSpec((block, width), lambda i: (i, 0)),
        ],
        out_specs=pl.BlockSpec((cols, width), lambda i: (0, 0)),
        scratch_shapes=[pltpu.VMEM((width, cols), F32)],
        compiler_params=pltpu.CompilerParams(vmem_limit_bytes=VMEM_LIMIT),
        cost_estimate=pl.CostEstimate(
            flops=6 * rows * cols * width,
            bytes_accessed=4 * rows * (cols + width),
            transcendentals=0,
        ),
    )(matrix, vec_rows)


def update_kernel(matrix_ref, vec_ref, image_ref, vec_side_ref, image_side_ref, out_ref, high, low):
    width = vec_ref.shape[1]

    @pl.when(pl.program_id(0) == 0)
    def _():
        high[:width, :], low[:width, :] = split(vec_side_ref[...].T)
        high[width:, :], low[width:, :] = split(image_side_ref[...].T)

    product = dot3(split(vec_ref[...]), (high[:width, :], low[:width, :]))
    product += dot3(split(image_ref[...]), (high[width:, :], low[width:, :]))
    out_ref[...] = matrix_ref[...] - product


def update(matrix, vec_rows, image_rows, vec_side, image_side):
    (rows, cols), width = matrix.shape, vec_rows.shape[1]
    block = min(512, rows)
    row_block = lambda size: pl.BlockSpec((block, size), lambda i: (i, 0))
    whole = pl.BlockSpec((cols, width), lambda i: (0, 0))
    return pl.pallas_call(
        update_kernel,
        grid=(rows // block,),
        out_shape=jax.ShapeDtypeStruct((rows, cols), F32),
        in_specs=[row_block(cols), row_block(width), row_block(width), whole, whole],
        out_specs=row_block(cols),
        scratch_shapes=[pltpu.VMEM((2 * width, cols), BF16)] * 2,
        compiler_params=pltpu.CompilerParams(vmem_limit_bytes=VMEM_LIMIT),
        cost_estimate=pl.CostEstimate(
            flops=12 * rows * cols * width,
            bytes_accessed=8 * rows * (cols + width),
            transcendentals=0,
        ),
    )(matrix, vec_rows, image_rows, vec_side, image_side)


def shifted(value, n_rows, step):
    return lax.ppermute(value, "row", [(i, (i + step) % n_rows) for i in range(n_rows)])


def gather_row(value, n_rows):
    parts = jnp.stack([value] + [shifted(value, n_rows, step) for step in range(1, n_rows)])
    row = lax.axis_index("row")
    ordered = [
        lax.dynamic_index_in_dim(parts, (row + n_rows - i) % n_rows, 0, keepdims=False)
        for i in range(n_rows)
    ]
    return jnp.concatenate(ordered, axis=0)


def sum_row(value, n_rows):
    return sum((shifted(value, n_rows, step) for step in range(1, n_rows)), value)


def scatter_row(value, n_rows):
    row = lax.axis_index("row")
    size = value.shape[0] // n_rows
    share = lambda i: lax.dynamic_slice_in_dim(value, i % n_rows * size, size, 0)
    total = share(row)
    for step in range(1, n_rows):
        total = total + shifted(share(row + step), n_rows, step)
    return total


def gather_col(value):
    return lax.all_gather(value, "col", axis=0, tiled=True)


def on_device(n_rows, n_cols, matrix, reflectors, factor):
    devices = [(r * n_cols + c, c * n_rows + r) for r in range(n_rows) for c in range(n_cols)]
    vec_rows = gather_col(reflectors)
    vec_share = lax.ppermute(reflectors, ("row", "col"), [(b, d) for d, b in devices])
    vec_cols = gather_row(vec_share, n_rows)

    image_share = scatter_row(image_part(matrix, vec_rows), n_rows)
    image_cols = gather_row(image_share, n_rows)
    image = lax.ppermute(image_share, ("row", "col"), devices)
    image_rows = gather_col(image)

    gram = sum_row(mult(vec_rows, image_rows, ((0,), (0,))), n_rows)
    inner = mult(mult(factor, gram, ((0,), (0,))), factor)
    correction = mult(image, factor) - 0.5 * mult(reflectors, inner)
    vec_side = mult(image_cols, factor) - 0.5 * mult(vec_cols, inner + inner.T)
    image_side = mult(vec_cols, factor, ((1,), (1,)))
    updated = update(matrix, vec_rows, image_rows, vec_side, image_side)
    return updated, correction


def solution(mesh):
    return jax.shard_map(
        functools.partial(on_device, mesh.shape["row"], mesh.shape["col"]),
        mesh=mesh,
        in_specs=(P("row", "col"), P(("row", "col"), None), P()),
        out_specs=(P("row", "col"), P(("row", "col"), None)),
        check_vma=False,
    )
```

```python
import functools

import jax
import jax.numpy as jnp
from jax import lax
from jax.experimental import pallas as pl
from jax.experimental.pallas import tpu as pltpu
from jax.sharding import PartitionSpec as P

F32 = jnp.float32
BF16 = jnp.bfloat16
VMEM_LIMIT = 48 * 1024 * 1024
GATHER_VMEM_LIMIT = 56 * 1024 * 1024


def split(value):
    high = value.astype(BF16)
    return high, (value - high.astype(F32)).astype(BF16)


def dot3(left, right):
    (left_high, left_low), (right_high, right_low) = left, right
    return jnp.dot(
        jnp.concatenate([left_high, left_low, left_high], axis=1),
        jnp.concatenate([right_high, right_high, right_low], axis=0),
        preferred_element_type=F32,
    )


def mult(left, right, dims=((1,), (0,))):
    return lax.dot_general(
        left, right, (dims, ((), ())), precision=lax.Precision.HIGH, preferred_element_type=F32
    )


def signed(index):
    return (index + 1) // 2 * (1 - index % 2 * 2)


def gather_kernel(n_rows, n_cols, send_cols, left_ref, block_ref, *refs):
    if send_cols:
        out_ref, rows_ref, cols_ref, *refs = refs
    else:
        out_ref, rows_ref, *refs = refs
    held, left, total, send_sem, recv_sem, left_sem, rows_sem, own_sem, *refs = refs
    n_chips = n_cols // 2
    near = 1 << (n_chips.bit_length() - 1) // 2
    far = n_chips // near
    row, me = lax.axis_index("row"), lax.axis_index("col")
    my_far, my_near, my_core = me // (2 * near), me // 2 % near, me % 2
    size = block_ref.shape[0]

    def at(far_pos, near_pos, core):
        return (far_pos * near + near_pos) * 2 + core

    neighbours = [
        (my_far + 1 < far, at(my_far + 1, my_near, my_core)),
        (my_far > 0, at(my_far - 1, my_near, my_core)),
        (my_near + 1 < near, at(my_far, my_near + 1, my_core)),
        (my_near > 0, at(my_far, my_near - 1, my_core)),
        (my_core >= 0, at(my_far, my_near, 1 - my_core)),
    ]

    def load(slot):
        rows = pl.ds(pl.multiple_of(slot * size, size), size)
        return pltpu.make_async_copy(left_ref.at[rows, :], left.at[slot], left_sem.at[slot])

    def store(slot):
        return pltpu.make_async_copy(held.at[slot], rows_ref.at[slot], rows_sem.at[slot])

    def send(index, slot):
        return pltpu.make_async_remote_copy(
            src_ref=held.at[slot],
            dst_ref=held.at[slot],
            send_sem=send_sem.at[index, slot],
            recv_sem=recv_sem.at[slot],
            device_id={"col": neighbours[index][1]},
            device_id_type=pl.DeviceIdType.MESH,
        )

    def sends(slot, far_pos, near_pos, core):
        same = core == my_core
        line = same & (near_pos == my_near)
        passes = [
            line & (far_pos <= my_far),
            line & (far_pos >= my_far),
            same & (near_pos <= my_near),
            same & (near_pos >= my_near),
            same,
        ]
        return [(neighbours[i][0] & passes[i], send(i, slot)) for i in range(5)]

    own_copy = pltpu.make_async_copy(block_ref, held.at[me], own_sem)
    own_copy.start()
    load(me).start()

    barrier = pltpu.get_barrier_semaphore()
    count = 0
    for there, device in neighbours:
        count = count + there.astype(jnp.int32)

        @pl.when(there)
        def _(device=device):
            pl.semaphore_signal(
                barrier, inc=1, device_id={"col": device}, device_id_type=pl.DeviceIdType.MESH
            )

    if send_cols:
        for step in range(1, n_rows):
            pl.semaphore_signal(
                barrier,
                inc=1,
                device_id={"row": (row + step) % n_rows},
                device_id_type=pl.DeviceIdType.MESH,
            )
        count = count + (n_rows - 1)
    pl.semaphore_wait(barrier, count)
    own_copy.wait()

    @pl.loop(0, n_cols)
    def _(slot):
        @pl.when(slot != me)
        def _():
            load(slot).start()

    if send_cols:
        cols_send_sem, cols_recv_sem, cols_own_sem = refs
        n_cols_rows = n_rows * size
        owner = me * n_rows // n_cols
        offset = pl.multiple_of(me * n_rows % n_cols * size, n_cols_rows)
        mine = left_ref.at[pl.ds(offset, n_cols_rows), :]
        cols_own = pltpu.make_async_copy(mine, cols_ref, cols_own_sem)
        cols_copies = [
            pltpu.make_async_remote_copy(
                src_ref=mine,
                dst_ref=cols_ref,
                send_sem=cols_send_sem.at[step - 1],
                recv_sem=cols_recv_sem,
                device_id={"row": (row + step) % n_rows},
                device_id_type=pl.DeviceIdType.MESH,
            )
            for step in range(1, n_rows)
        ]

        @pl.when(row == owner)
        def _():
            cols_own.start()
            for copy in cols_copies:
                copy.start()

    total[...] = jnp.zeros_like(total)
    n_near = 2 * near - 1

    @pl.loop(0, (far + 1) * n_near * 4)
    def _(step):
        distance = step // (4 * n_near) - (step // 4 % n_near > 0).astype(jnp.int32)
        far_pos = my_far + distance * (1 - step % 2 * 2)
        near_pos = my_near + signed(step // 4 % n_near)
        core = (my_core + step // 2) % 2
        valid = (distance >= 0) & (distance < far) & ((distance > 0) | (step % 2 == 0))
        valid &= (far_pos >= 0) & (far_pos < far) & (near_pos >= 0) & (near_pos < near)

        @pl.when(valid)
        def _():
            slot = at(far_pos, near_pos, core)

            @pl.when(slot != me)
            def _():
                send(4, slot).wait_recv()

            for passed, copy in sends(slot, far_pos, near_pos, core):
                pl.when(passed)(copy.start)
            store(slot).start()
            load(slot).wait()
            total[...] += dot3(split(held[slot].T), split(left[slot]))

    out_ref[...] = total[...].T

    @pl.loop(0, n_cols)
    def _(slot):
        for passed, copy in sends(slot, slot // (2 * near), slot // 2 % near, slot % 2):
            pl.when(passed)(copy.wait_send)
        store(slot).wait()

    if send_cols:

        @pl.when(row == owner)
        def _():
            cols_own.wait()
            for copy in cols_copies:
                copy.wait_send()

        @pl.when(row != owner)
        def _():
            cols_copies[0].wait_recv()


def gather_product(left, block, n_rows, n_cols, send_cols):
    (rows, cols), (size, width) = left.shape, block.shape
    shapes = [(cols, width), (n_cols, size, width)] + [(n_rows * size, cols)] * send_cols
    in_hbm = pl.BlockSpec(memory_space=pl.ANY)
    in_vmem = pl.BlockSpec(memory_space=pltpu.VMEM)
    dma = pltpu.SemaphoreType.DMA
    product, gathered, *rest = pl.pallas_call(
        functools.partial(gather_kernel, n_rows, n_cols, send_cols),
        out_shape=[jax.ShapeDtypeStruct(shape, F32) for shape in shapes],
        in_specs=[in_hbm, in_hbm],
        out_specs=[in_vmem, in_hbm] + [in_hbm] * send_cols,
        scratch_shapes=[
            pltpu.VMEM((n_cols, size, width), F32),
            pltpu.VMEM((n_cols, size, cols), F32),
            pltpu.VMEM((width, cols), F32),
            dma((5, n_cols)),
            dma((n_cols,)),
            dma((n_cols,)),
            dma((n_cols,)),
            dma,
        ]
        + [dma((n_rows - 1,)), dma, dma] * send_cols,
        compiler_params=pltpu.CompilerParams(
            collective_id=int(send_cols), has_side_effects=True, vmem_limit_bytes=GATHER_VMEM_LIMIT
        ),
        cost_estimate=pl.CostEstimate(
            flops=6 * rows * cols * width,
            bytes_accessed=4 * rows * (cols + width),
            transcendentals=0,
        ),
    )(left, block)
    return product, gathered.reshape(rows, width), *rest


def update_kernel(matrix_ref, vec_ref, image_ref, vec_side_ref, image_side_ref, out_ref, high, low):
    width = vec_ref.shape[1]

    @pl.when(pl.program_id(0) == 0)
    def _():
        high[:width, :], low[:width, :] = split(vec_side_ref[...].T)
        high[width:, :], low[width:, :] = split(image_side_ref[...].T)

    product = dot3(split(vec_ref[...]), (high[:width, :], low[:width, :]))
    product += dot3(split(image_ref[...]), (high[width:, :], low[width:, :]))
    out_ref[...] = matrix_ref[...] - product


def update(matrix, vec_rows, image_rows, vec_side, image_side):
    (rows, cols), width = matrix.shape, vec_rows.shape[1]
    block = min(512, rows)
    row_block = lambda size: pl.BlockSpec((block, size), lambda i: (i, 0))
    whole = pl.BlockSpec((cols, width), lambda i: (0, 0))
    return pl.pallas_call(
        update_kernel,
        grid=(rows // block,),
        out_shape=jax.ShapeDtypeStruct((rows, cols), F32),
        in_specs=[row_block(cols), row_block(width), row_block(width), whole, whole],
        out_specs=row_block(cols),
        scratch_shapes=[pltpu.VMEM((2 * width, cols), BF16)] * 2,
        compiler_params=pltpu.CompilerParams(vmem_limit_bytes=VMEM_LIMIT),
        cost_estimate=pl.CostEstimate(
            flops=12 * rows * cols * width,
            bytes_accessed=8 * rows * (cols + width),
            transcendentals=0,
        ),
    )(matrix, vec_rows, image_rows, vec_side, image_side)


def shifted(value, n_rows, step):
    return lax.ppermute(value, "row", [(i, (i + step) % n_rows) for i in range(n_rows)])


def gather_row(value, n_rows):
    parts = jnp.stack([value] + [shifted(value, n_rows, step) for step in range(1, n_rows)])
    row = lax.axis_index("row")
    ordered = [
        lax.dynamic_index_in_dim(parts, (row + n_rows - i) % n_rows, 0, keepdims=False)
        for i in range(n_rows)
    ]
    return jnp.concatenate(ordered, axis=0)


def sum_row(value, n_rows):
    return sum((shifted(value, n_rows, step) for step in range(1, n_rows)), value)


def scatter_row(value, n_rows):
    row = lax.axis_index("row")
    size = value.shape[0] // n_rows
    share = lambda i: lax.dynamic_slice_in_dim(value, i % n_rows * size, size, 0)
    total = share(row)
    for step in range(1, n_rows):
        total = total + shifted(share(row + step), n_rows, step)
    return total


def on_device(n_rows, n_cols, matrix, reflectors, factor):
    devices = [(r * n_cols + c, c * n_rows + r) for r in range(n_rows) for c in range(n_cols)]
    image_term, vec_rows = gather_product(matrix, reflectors, n_rows, n_cols, False)
    image_share = scatter_row(image_term, n_rows)
    image = lax.ppermute(image_share, ("row", "col"), devices)
    gram_term, image_rows, vec_cols = gather_product(vec_rows, image, n_rows, n_cols, True)
    image_cols = gather_row(image_share, n_rows)

    gram = sum_row(gram_term, n_rows)
    inner = mult(mult(factor, gram, ((0,), (0,))), factor)
    correction = mult(image, factor) - 0.5 * mult(reflectors, inner)
    vec_side = mult(image_cols, factor) - 0.5 * mult(vec_cols, inner + inner.T)
    image_side = mult(vec_cols, factor, ((1,), (1,)))
    updated = update(matrix, vec_rows, image_rows, vec_side, image_side)
    return updated, correction


def solution(mesh):
    return jax.shard_map(
        functools.partial(on_device, mesh.shape["row"], mesh.shape["col"]),
        mesh=mesh,
        in_specs=(P("row", "col"), P(("row", "col"), None), P()),
        out_specs=(P("row", "col"), P(("row", "col"), None)),
        check_vma=False,
    )
```

```python
import functools

import jax
import jax.numpy as jnp
from jax import lax
from jax.experimental import pallas as pl
from jax.experimental.pallas import tpu as pltpu
from jax.sharding import PartitionSpec as P

F32 = jnp.float32
BF16 = jnp.bfloat16
VMEM_LIMIT = 48 * 1024 * 1024
GATHER_VMEM_LIMIT = 56 * 1024 * 1024


def split(value):
    high = value.astype(BF16)
    return high, (value - high.astype(F32)).astype(BF16)


def dot3(left, right):
    (left_high, left_low), (right_high, right_low) = left, right
    return jnp.dot(
        jnp.concatenate([left_high, left_low, left_high], axis=1),
        jnp.concatenate([right_high, right_high, right_low], axis=0),
        preferred_element_type=F32,
    )


def mult(left, right, dims=((1,), (0,))):
    return lax.dot_general(
        left, right, (dims, ((), ())), precision=lax.Precision.HIGH, preferred_element_type=F32
    )


def signed(index):
    return (index + 1) // 2 * (1 - index % 2 * 2)


def gather_kernel(n_rows, n_cols, send_cols, left_ref, block_ref, *refs):
    if send_cols:
        out_ref, rows_ref, cols_ref, sum_ref, *refs = refs
    else:
        out_ref, rows_ref, *refs = refs
    held, left, total, send_sem, recv_sem, left_sem, rows_sem, own_sem, *refs = refs
    n_chips = n_cols // 2
    near = 1 << (n_chips.bit_length() - 1) // 2
    far = n_chips // near
    row, me = lax.axis_index("row"), lax.axis_index("col")
    my_far, my_near, my_core = me // (2 * near), me // 2 % near, me % 2
    size = held.shape[1]

    def at(far_pos, near_pos, core):
        return (far_pos * near + near_pos) * 2 + core

    neighbours = [
        (my_far + 1 < far, at(my_far + 1, my_near, my_core)),
        (my_far > 0, at(my_far - 1, my_near, my_core)),
        (my_near + 1 < near, at(my_far, my_near + 1, my_core)),
        (my_near > 0, at(my_far, my_near - 1, my_core)),
        (my_core >= 0, at(my_far, my_near, 1 - my_core)),
    ]

    def load(slot):
        rows = pl.ds(pl.multiple_of(slot * size, size), size)
        return pltpu.make_async_copy(left_ref.at[rows, :], left.at[slot], left_sem.at[slot])

    def store(slot):
        return pltpu.make_async_copy(held.at[slot], rows_ref.at[slot], rows_sem.at[slot])

    def send(index, slot):
        return pltpu.make_async_remote_copy(
            src_ref=held.at[slot],
            dst_ref=held.at[slot],
            send_sem=send_sem.at[index, slot],
            recv_sem=recv_sem.at[slot],
            device_id={"col": neighbours[index][1]},
            device_id_type=pl.DeviceIdType.MESH,
        )

    def sends(slot, far_pos, near_pos, core):
        same = core == my_core
        line = same & (near_pos == my_near)
        passes = [
            line & (far_pos <= my_far),
            line & (far_pos >= my_far),
            same & (near_pos <= my_near),
            same & (near_pos >= my_near),
            same,
        ]
        return [(neighbours[i][0] & passes[i], send(i, slot)) for i in range(5)]

    if not send_cols:
        own_copy = pltpu.make_async_copy(block_ref, held.at[me], own_sem)
        own_copy.start()
    load(me).start()

    barrier = pltpu.get_barrier_semaphore()
    count = 0
    for there, device in neighbours:
        count = count + there.astype(jnp.int32)

        @pl.when(there)
        def _(device=device):
            pl.semaphore_signal(
                barrier, inc=1, device_id={"col": device}, device_id_type=pl.DeviceIdType.MESH
            )

    if send_cols:
        for step in range(1, n_rows):
            pl.semaphore_signal(
                barrier,
                inc=1,
                device_id={"row": (row + step) % n_rows},
                device_id_type=pl.DeviceIdType.MESH,
            )
        flat = row * n_cols + me
        source_col = flat // n_rows
        for source_row in range(n_rows):

            @pl.when(source_row * n_cols + source_col != flat)
            def _(source_row=source_row):
                pl.semaphore_signal(
                    barrier,
                    inc=1,
                    device_id={"row": source_row, "col": source_col},
                    device_id_type=pl.DeviceIdType.MESH,
                )

        count = count + (2 * n_rows - 1) - (source_col == me).astype(jnp.int32)
    pl.semaphore_wait(barrier, count)
    if send_cols:
        cols_send_sem, cols_recv_sem, cols_own_sem, *refs = refs
        shares, peers, grams, gram_own, *refs = refs
        share_send, share_recv, peer_send, peer_recv, gram_send, gram_recv = refs
        targets = [me * n_rows + i for i in range(n_rows)]

        def share_copy(i):
            return pltpu.make_async_remote_copy(
                src_ref=block_ref.at[pl.ds(i * size, size), :],
                dst_ref=shares.at[row],
                send_sem=share_send.at[i],
                recv_sem=share_recv.at[row],
                device_id={"row": targets[i] // n_cols, "col": targets[i] % n_cols},
                device_id_type=pl.DeviceIdType.MESH,
            )

        def share_own(i):
            return pltpu.make_async_copy(
                block_ref.at[pl.ds(i * size, size), :], shares.at[row], own_sem
            )

        for i in range(n_rows):
            pl.when(targets[i] != flat)(share_copy(i).start)
            pl.when(targets[i] == flat)(share_own(i).start)
        for i in range(n_rows):
            pl.when(targets[i] == flat)(share_own(i).wait)

            @pl.when(i * n_cols + source_col != flat)
            def _(i=i):
                pltpu.make_async_remote_copy(
                    src_ref=shares.at[i],
                    dst_ref=shares.at[i],
                    send_sem=share_send.at[i],
                    recv_sem=share_recv.at[i],
                    device_id={"row": targets[i] // n_cols, "col": targets[i] % n_cols},
                    device_id_type=pl.DeviceIdType.MESH,
                ).wait_recv()

        held[me] = sum((shares[i] for i in range(1, n_rows)), shares[0])

        def to_row(source, target, send_sems, recv_sems, step):
            return pltpu.make_async_remote_copy(
                src_ref=source,
                dst_ref=target.at[step - 1],
                send_sem=send_sems.at[step - 1],
                recv_sem=recv_sems.at[step - 1],
                device_id={"row": (row + step) % n_rows},
                device_id_type=pl.DeviceIdType.MESH,
            )

        peer_copies = [
            to_row(block_ref, peers, peer_send, peer_recv, step) for step in range(1, n_rows)
        ]
        gram_copies = [
            to_row(gram_own, grams, gram_send, gram_recv, step) for step in range(1, n_rows)
        ]
    else:
        own_copy.wait()

    @pl.loop(0, n_cols)
    def _(slot):
        @pl.when(slot != me)
        def _():
            load(slot).start()

    if send_cols:
        n_cols_rows = n_rows * size
        owner = me * n_rows // n_cols
        offset = pl.multiple_of(me * n_rows % n_cols * size, n_cols_rows)
        mine = left_ref.at[pl.ds(offset, n_cols_rows), :]
        cols_own = pltpu.make_async_copy(mine, cols_ref, cols_own_sem)
        cols_copies = [
            pltpu.make_async_remote_copy(
                src_ref=mine,
                dst_ref=cols_ref,
                send_sem=cols_send_sem.at[step - 1],
                recv_sem=cols_recv_sem,
                device_id={"row": (row + step) % n_rows},
                device_id_type=pl.DeviceIdType.MESH,
            )
            for step in range(1, n_rows)
        ]

        @pl.when(row == owner)
        def _():
            cols_own.start()
            for copy in cols_copies:
                copy.start()

        for copy in peer_copies:
            copy.start()

    total[...] = jnp.zeros_like(total)
    n_near = 2 * near - 1

    @pl.loop(0, (far + 1) * n_near * 4)
    def _(step):
        distance = step // (4 * n_near) - (step // 4 % n_near > 0).astype(jnp.int32)
        far_pos = my_far + distance * (1 - step % 2 * 2)
        near_pos = my_near + signed(step // 4 % n_near)
        core = (my_core + step // 2) % 2
        valid = (distance >= 0) & (distance < far) & ((distance > 0) | (step % 2 == 0))
        valid &= (far_pos >= 0) & (far_pos < far) & (near_pos >= 0) & (near_pos < near)

        @pl.when(valid)
        def _():
            slot = at(far_pos, near_pos, core)

            @pl.when(slot != me)
            def _():
                send(4, slot).wait_recv()

            for passed, copy in sends(slot, far_pos, near_pos, core):
                pl.when(passed)(copy.start)
            store(slot).start()
            load(slot).wait()
            total[...] += dot3(split(held[slot].T), split(left[slot]))

    if send_cols:
        gram_own[...] = total[...].T
        for copy in gram_copies:
            copy.start()
    else:
        out_ref[...] = total[...].T

    @pl.loop(0, n_cols)
    def _(slot):
        for passed, copy in sends(slot, slot // (2 * near), slot // 2 % near, slot % 2):
            pl.when(passed)(copy.wait_send)
        store(slot).wait()

    if send_cols:

        @pl.when(row == owner)
        def _():
            cols_own.wait()
            for copy in cols_copies:
                copy.wait_send()

        @pl.when(row != owner)
        def _():
            cols_copies[0].wait_recv()

        for i in range(n_rows):
            pl.when(targets[i] != flat)(share_copy(i).wait_send)
        for copy in peer_copies + gram_copies:
            copy.wait()
        sum_ref[...] = sum((peers[i] for i in range(n_rows - 1)), block_ref[...])
        out_ref[...] = sum((grams[i] for i in range(n_rows - 1)), gram_own[...])


def gather_product(left, block, n_rows, n_cols, send_cols):
    (rows, cols), width = left.shape, block.shape[1]
    size = rows // n_cols
    shapes = [(cols, width), (n_cols, size, width)]
    shapes += [(n_rows * size, cols), (n_rows * size, width)] * send_cols
    in_hbm = pl.BlockSpec(memory_space=pl.ANY)
    in_vmem = pl.BlockSpec(memory_space=pltpu.VMEM)
    dma = pltpu.SemaphoreType.DMA
    product, gathered, *rest = pl.pallas_call(
        functools.partial(gather_kernel, n_rows, n_cols, send_cols),
        out_shape=[jax.ShapeDtypeStruct(shape, F32) for shape in shapes],
        in_specs=[in_hbm, in_vmem if send_cols else in_hbm],
        out_specs=[in_vmem, in_hbm] + [in_hbm, in_vmem] * send_cols,
        scratch_shapes=[
            pltpu.VMEM((n_cols, size, width), F32),
            pltpu.VMEM((n_cols, size, cols), F32),
            pltpu.VMEM((width, cols), F32),
            dma((5, n_cols)),
            dma((n_cols,)),
            dma((n_cols,)),
            dma((n_cols,)),
            dma,
        ]
        + [
            dma((n_rows - 1,)),
            dma,
            dma,
            pltpu.VMEM((n_rows, size, width), F32),
            pltpu.VMEM((n_rows - 1, n_rows * size, width), F32),
            pltpu.VMEM((n_rows - 1, cols, width), F32),
            pltpu.VMEM((cols, width), F32),
            dma((n_rows,)),
            dma((n_rows,)),
        ]
        * send_cols
        + [dma((n_rows - 1,))] * (4 * send_cols),
        compiler_params=pltpu.CompilerParams(
            collective_id=int(send_cols), has_side_effects=True, vmem_limit_bytes=GATHER_VMEM_LIMIT
        ),
        cost_estimate=pl.CostEstimate(
            flops=6 * rows * cols * width,
            bytes_accessed=4 * rows * (cols + width),
            transcendentals=0,
        ),
    )(left, block)
    return product, gathered.reshape(rows, width), *rest


def update_kernel(matrix_ref, vec_ref, image_ref, vec_side_ref, image_side_ref, out_ref, sides):
    width = vec_ref.shape[1]

    @pl.when(pl.program_id(0) == 0)
    def _():
        for i, side_ref in enumerate((vec_side_ref, image_side_ref)):
            high, low = split(side_ref[...].T)
            for j, part in enumerate((high, high, low)):
                sides[pl.ds((3 * i + j) * width, width), :] = part

    vec_high, vec_low = split(vec_ref[...])
    image_high, image_low = split(image_ref[...])
    parts = [vec_high, vec_low, vec_high, image_high, image_low, image_high]
    product = jnp.dot(
        jnp.concatenate(parts, axis=1), sides[...], preferred_element_type=F32
    )
    out_ref[...] = matrix_ref[...] - product


def update(matrix, vec_rows, image_rows, vec_side, image_side):
    (rows, cols), width = matrix.shape, vec_rows.shape[1]
    block = min(512, rows)
    row_block = lambda size: pl.BlockSpec((block, size), lambda i: (i, 0))
    whole = pl.BlockSpec((cols, width), lambda i: (0, 0))
    return pl.pallas_call(
        update_kernel,
        grid=(rows // block,),
        out_shape=jax.ShapeDtypeStruct((rows, cols), F32),
        in_specs=[row_block(cols), row_block(width), row_block(width), whole, whole],
        out_specs=row_block(cols),
        scratch_shapes=[pltpu.VMEM((6 * width, cols), BF16)],
        compiler_params=pltpu.CompilerParams(vmem_limit_bytes=VMEM_LIMIT),
        cost_estimate=pl.CostEstimate(
            flops=12 * rows * cols * width,
            bytes_accessed=8 * rows * (cols + width),
            transcendentals=0,
        ),
    )(matrix, vec_rows, image_rows, vec_side, image_side)


def on_device(n_rows, n_cols, matrix, reflectors, factor):
    image_term, vec_rows = gather_product(matrix, reflectors, n_rows, n_cols, False)
    gram, image_rows, vec_cols, image_cols = gather_product(
        vec_rows, image_term, n_rows, n_cols, True
    )
    size = reflectors.shape[0]
    image = lax.dynamic_slice_in_dim(image_rows, lax.axis_index("col") * size, size, 0)
    inner = mult(mult(factor, gram, ((0,), (0,))), factor)
    correction = mult(image, factor) - 0.5 * mult(reflectors, inner)
    vec_side = mult(image_cols, factor) - 0.5 * mult(vec_cols, inner + inner.T)
    image_side = mult(vec_cols, factor, ((1,), (1,)))
    updated = update(matrix, vec_rows, image_rows, vec_side, image_side)
    return updated, correction


def solution(mesh):
    return jax.shard_map(
        functools.partial(on_device, mesh.shape["row"], mesh.shape["col"]),
        mesh=mesh,
        in_specs=(P("row", "col"), P(("row", "col"), None), P()),
        out_specs=(P("row", "col"), P(("row", "col"), None)),
        check_vma=False,
    )
```

```python
import functools

import jax
import jax.numpy as jnp
from jax import lax
from jax.experimental import pallas as pl
from jax.experimental.pallas import tpu as pltpu
from jax.sharding import PartitionSpec as P

F32 = jnp.float32
BF16 = jnp.bfloat16
MIB = 1024 * 1024
LINK_WEIGHT = 16


def split(value):
    high = value.astype(BF16)
    return high, (value - high.astype(F32)).astype(BF16)


def dot3(left, right):
    (left_high, left_low), (right_high, right_low) = left, right
    return jnp.dot(
        jnp.concatenate([left_high, left_low, left_high], axis=1),
        jnp.concatenate([right_high, right_high, right_low], axis=0),
        preferred_element_type=F32,
    )


def mult(left, right, dims=((1,), (0,))):
    return lax.dot_general(
        left, right, (dims, ((), ())), precision=lax.Precision.HIGH, preferred_element_type=F32
    )


def signed(index):
    return (index + 1) // 2 * (1 - index % 2 * 2)


def gather_kernel(n_rows, n_cols, send_cols, left_ref, block_ref, *refs):
    if send_cols:
        out_ref, rows_ref, cols_ref, sum_ref, *refs = refs
    else:
        out_ref, rows_ref, *refs = refs
    held, left, total, send_sem, recv_sem, left_sem, rows_sem, own_sem, *refs = refs
    n_chips = n_cols // 2
    near = 1 << (n_chips.bit_length() - 1) // 2
    far = n_chips // near
    row, me = lax.axis_index("row"), lax.axis_index("col")
    my_far, my_near, my_core = me // (2 * near), me // 2 % near, me % 2
    size = held.shape[1]

    def at(far_pos, near_pos, core):
        return (far_pos * near + near_pos) * 2 + core

    neighbours = [
        (my_far + 1 < far, at(my_far + 1, my_near, my_core)),
        (my_far > 0, at(my_far - 1, my_near, my_core)),
        (my_near + 1 < near, at(my_far, my_near + 1, my_core)),
        (my_near > 0, at(my_far, my_near - 1, my_core)),
        (my_core >= 0, at(my_far, my_near, 1 - my_core)),
    ]

    def load(slot):
        rows = pl.ds(pl.multiple_of(slot * size, size), size)
        return pltpu.make_async_copy(left_ref.at[rows, :], left.at[slot], left_sem.at[slot])

    def store(slot):
        return pltpu.make_async_copy(held.at[slot], rows_ref.at[slot], rows_sem.at[slot])

    def send(index, slot):
        return pltpu.make_async_remote_copy(
            src_ref=held.at[slot],
            dst_ref=held.at[slot],
            send_sem=send_sem.at[index, slot],
            recv_sem=recv_sem.at[slot],
            device_id={"col": neighbours[index][1]},
            device_id_type=pl.DeviceIdType.MESH,
        )

    def sends(slot, far_pos, near_pos, core):
        same = core == my_core
        line = same & (near_pos == my_near)
        passes = [
            line & (far_pos <= my_far),
            line & (far_pos >= my_far),
            same & (near_pos <= my_near),
            same & (near_pos >= my_near),
            same,
        ]
        return [(neighbours[i][0] & passes[i], send(i, slot)) for i in range(5)]

    if not send_cols:
        own_copy = pltpu.make_async_copy(block_ref, held.at[me], own_sem)
        own_copy.start()
    load(me).start()

    barrier = pltpu.get_barrier_semaphore()
    count = 0
    for there, device in neighbours:
        count = count + there.astype(jnp.int32)

        @pl.when(there)
        def _(device=device):
            pl.semaphore_signal(
                barrier, inc=1, device_id={"col": device}, device_id_type=pl.DeviceIdType.MESH
            )

    if send_cols:
        for step in range(1, n_rows):
            pl.semaphore_signal(
                barrier,
                inc=1,
                device_id={"row": (row + step) % n_rows},
                device_id_type=pl.DeviceIdType.MESH,
            )
        flat = row * n_cols + me
        source_col = flat // n_rows
        for source_row in range(n_rows):

            @pl.when(source_row * n_cols + source_col != flat)
            def _(source_row=source_row):
                pl.semaphore_signal(
                    barrier,
                    inc=1,
                    device_id={"row": source_row, "col": source_col},
                    device_id_type=pl.DeviceIdType.MESH,
                )

        count = count + (2 * n_rows - 1) - (source_col == me).astype(jnp.int32)
    pl.semaphore_wait(barrier, count)
    if send_cols:
        cols_send_sem, cols_recv_sem, cols_own_sem, *refs = refs
        shares, peers, grams, gram_own, *refs = refs
        share_send, share_recv, peer_send, peer_recv, gram_send, gram_recv = refs
        targets = [me * n_rows + i for i in range(n_rows)]

        def share_copy(i):
            return pltpu.make_async_remote_copy(
                src_ref=block_ref.at[pl.ds(i * size, size), :],
                dst_ref=shares.at[row],
                send_sem=share_send.at[i],
                recv_sem=share_recv.at[row],
                device_id={"row": targets[i] // n_cols, "col": targets[i] % n_cols},
                device_id_type=pl.DeviceIdType.MESH,
            )

        def share_own(i):
            return pltpu.make_async_copy(
                block_ref.at[pl.ds(i * size, size), :], shares.at[row], own_sem
            )

        for i in range(n_rows):
            pl.when(targets[i] != flat)(share_copy(i).start)
            pl.when(targets[i] == flat)(share_own(i).start)
        for i in range(n_rows):
            pl.when(targets[i] == flat)(share_own(i).wait)

            @pl.when(i * n_cols + source_col != flat)
            def _(i=i):
                pltpu.make_async_remote_copy(
                    src_ref=shares.at[i],
                    dst_ref=shares.at[i],
                    send_sem=share_send.at[i],
                    recv_sem=share_recv.at[i],
                    device_id={"row": targets[i] // n_cols, "col": targets[i] % n_cols},
                    device_id_type=pl.DeviceIdType.MESH,
                ).wait_recv()

        held[me] = sum((shares[i] for i in range(1, n_rows)), shares[0])

        def to_row(source, target, send_sems, recv_sems, step):
            return pltpu.make_async_remote_copy(
                src_ref=source,
                dst_ref=target.at[step - 1],
                send_sem=send_sems.at[step - 1],
                recv_sem=recv_sems.at[step - 1],
                device_id={"row": (row + step) % n_rows},
                device_id_type=pl.DeviceIdType.MESH,
            )

        peer_copies = [
            to_row(block_ref, peers, peer_send, peer_recv, step) for step in range(1, n_rows)
        ]
        gram_copies = [
            to_row(gram_own, grams, gram_send, gram_recv, step) for step in range(1, n_rows)
        ]
    else:
        own_copy.wait()

    @pl.loop(0, n_cols)
    def _(slot):
        @pl.when(slot != me)
        def _():
            load(slot).start()

    if send_cols:
        n_cols_rows = n_rows * size
        owner = me * n_rows // n_cols
        offset = pl.multiple_of(me * n_rows % n_cols * size, n_cols_rows)
        mine = left_ref.at[pl.ds(offset, n_cols_rows), :]
        cols_own = pltpu.make_async_copy(mine, cols_ref, cols_own_sem)
        cols_copies = [
            pltpu.make_async_remote_copy(
                src_ref=mine,
                dst_ref=cols_ref,
                send_sem=cols_send_sem.at[step - 1],
                recv_sem=cols_recv_sem,
                device_id={"row": (row + step) % n_rows},
                device_id_type=pl.DeviceIdType.MESH,
            )
            for step in range(1, n_rows)
        ]

        @pl.when(row == owner)
        def _():
            cols_own.start()
            for copy in cols_copies:
                copy.start()

        for copy in peer_copies:
            copy.start()

    total[...] = jnp.zeros_like(total)
    n_near = 2 * near - 1

    @pl.loop(0, (far + 1) * n_near * 4)
    def _(step):
        distance = step // (4 * n_near) - (step // 4 % n_near > 0).astype(jnp.int32)
        far_pos = my_far + distance * (1 - step % 2 * 2)
        near_pos = my_near + signed(step // 4 % n_near)
        core = (my_core + step // 2) % 2
        valid = (distance >= 0) & (distance < far) & ((distance > 0) | (step % 2 == 0))
        valid &= (far_pos >= 0) & (far_pos < far) & (near_pos >= 0) & (near_pos < near)

        @pl.when(valid)
        def _():
            slot = at(far_pos, near_pos, core)

            @pl.when(slot != me)
            def _():
                send(4, slot).wait_recv()

            for passed, copy in sends(slot, far_pos, near_pos, core):
                pl.when(passed)(copy.start)
            store(slot).start()
            load(slot).wait()
            total[...] += dot3(split(held[slot].T), split(left[slot]))

    if send_cols:
        gram_own[...] = total[...].T
        for copy in gram_copies:
            copy.start()
    else:
        out_ref[...] = total[...].T

    @pl.loop(0, n_cols)
    def _(slot):
        for passed, copy in sends(slot, slot // (2 * near), slot // 2 % near, slot % 2):
            pl.when(passed)(copy.wait_send)
        store(slot).wait()

    if send_cols:

        @pl.when(row == owner)
        def _():
            cols_own.wait()
            for copy in cols_copies:
                copy.wait_send()

        @pl.when(row != owner)
        def _():
            cols_copies[0].wait_recv()

        for i in range(n_rows):
            pl.when(targets[i] != flat)(share_copy(i).wait_send)
        for copy in peer_copies + gram_copies:
            copy.wait()
        sum_ref[...] = sum((peers[i] for i in range(n_rows - 1)), block_ref[...])
        out_ref[...] = sum((grams[i] for i in range(n_rows - 1)), gram_own[...])


def gather_product(left, block, n_rows, n_cols, send_cols):
    (rows, cols), width = left.shape, block.shape[1]
    size = rows // n_cols
    shapes = [(cols, width), (n_cols, size, width)]
    shapes += [(n_rows * size, cols), (n_rows * size, width)] * send_cols
    in_hbm = pl.BlockSpec(memory_space=pl.ANY)
    in_vmem = pl.BlockSpec(memory_space=pltpu.VMEM)
    dma = pltpu.SemaphoreType.DMA
    product, gathered, *rest = pl.pallas_call(
        functools.partial(gather_kernel, n_rows, n_cols, send_cols),
        out_shape=[jax.ShapeDtypeStruct(shape, F32) for shape in shapes],
        in_specs=[
            pl.BlockSpec(memory_space=pltpu.HBM),
            in_vmem if send_cols else in_hbm,
        ],
        out_specs=[in_vmem, in_hbm] + [in_hbm, in_vmem] * send_cols,
        scratch_shapes=[
            pltpu.VMEM((n_cols, size, width), F32),
            pltpu.VMEM((n_cols, size, cols), F32),
            pltpu.VMEM((width, cols), F32),
            dma((5, n_cols)),
            dma((n_cols,)),
            dma((n_cols,)),
            dma((n_cols,)),
            dma,
        ]
        + [
            dma((n_rows - 1,)),
            dma,
            dma,
            pltpu.VMEM((n_rows, size, width), F32),
            pltpu.VMEM((n_rows - 1, n_rows * size, width), F32),
            pltpu.VMEM((n_rows - 1, cols, width), F32),
            pltpu.VMEM((cols, width), F32),
            dma((n_rows,)),
            dma((n_rows,)),
        ]
        * send_cols
        + [dma((n_rows - 1,))] * (4 * send_cols),
        compiler_params=pltpu.CompilerParams(
            collective_id=int(send_cols), has_side_effects=True, vmem_limit_bytes=(42 if send_cols else 56) * MIB
        ),
        cost_estimate=pl.CostEstimate(
            flops=6 * rows * cols * width,
            bytes_accessed=4 * rows * (cols + LINK_WEIGHT * width),
            transcendentals=0,
        ),
    )(left, block)
    return product, gathered.reshape(rows, width), *rest


def update_kernel(matrix_ref, vec_ref, image_ref, vec_side_ref, image_side_ref, out_ref, sides):
    width = vec_ref.shape[1]

    @pl.when(pl.program_id(0) == 0)
    def _():
        for i, side_ref in enumerate((vec_side_ref, image_side_ref)):
            high, low = split(side_ref[...].T)
            for j, part in enumerate((high, high, low)):
                sides[pl.ds((3 * i + j) * width, width), :] = part

    vec_high, vec_low = split(vec_ref[...])
    image_high, image_low = split(image_ref[...])
    parts = [vec_high, vec_low, vec_high, image_high, image_low, image_high]
    product = jnp.dot(
        jnp.concatenate(parts, axis=1), sides[...], preferred_element_type=F32
    )
    out_ref[...] = matrix_ref[...] - product


def update(matrix, vec_rows, image_rows, vec_side, image_side):
    (rows, cols), width = matrix.shape, vec_rows.shape[1]
    block = min(256, rows)
    row_block = lambda size: pl.BlockSpec((block, size), lambda i: (i, 0))
    whole = pl.BlockSpec((cols, width), lambda i: (0, 0))
    return pl.pallas_call(
        update_kernel,
        grid=(rows // block,),
        out_shape=jax.ShapeDtypeStruct((rows, cols), F32),
        in_specs=[row_block(cols), row_block(width), row_block(width), whole, whole],
        out_specs=row_block(cols),
        scratch_shapes=[pltpu.VMEM((6 * width, cols), BF16)],
        compiler_params=pltpu.CompilerParams(vmem_limit_bytes=20 * MIB),
        cost_estimate=pl.CostEstimate(
            flops=12 * rows * cols * width,
            bytes_accessed=8 * rows * (cols + width),
            transcendentals=0,
        ),
    )(matrix, vec_rows, image_rows, vec_side, image_side)


def on_device(n_rows, n_cols, matrix, reflectors, factor):
    image_term, vec_rows = gather_product(matrix, reflectors, n_rows, n_cols, False)
    gram, image_rows, vec_cols, image_cols = gather_product(
        vec_rows, image_term, n_rows, n_cols, True
    )
    size = reflectors.shape[0]
    image = lax.dynamic_slice_in_dim(image_rows, lax.axis_index("col") * size, size, 0)
    inner = mult(mult(factor, gram, ((0,), (0,))), factor)
    correction = mult(image, factor) - 0.5 * mult(reflectors, inner)
    vec_side = mult(image_cols, factor) - 0.5 * mult(vec_cols, inner + inner.T)
    image_side = mult(vec_cols, factor, ((1,), (1,)))
    updated = update(matrix, vec_rows, image_rows, vec_side, image_side)
    return updated, correction


def solution(mesh):
    return jax.shard_map(
        functools.partial(on_device, mesh.shape["row"], mesh.shape["col"]),
        mesh=mesh,
        in_specs=(P("row", "col"), P(("row", "col"), None), P()),
        out_specs=(P("row", "col"), P(("row", "col"), None)),
        check_vma=False,
    )
```
